32 devices in a mesh: groups: 2 (over x), seq: 8 (over z, y), slab: 2 (over core).
Axes of the slice: x: 2, y: 2, z: 4, core: 2. Of those that a mesh axis runs over, the one named last changes fastest.
Arguments:
- noise: float32 [128, 64], P(('groups', 'seq')), parts along dimension 0, may hold values from -6 to 6
- timesteps: int32 [4, 4], P('groups'), parts along dimension 0, may hold values from 0 to 999, as said below
- fine_counts: int32 [4], P('groups'), parts along dimension 0, may hold values from 1 to 3
- w_in: bfloat16 [64, 2560], replicated, may hold values from -0.75 to 0.75
- w_query: bfloat16 [2560, 1024], P(None, 'seq'), may hold values from -24 to 24
- w_key: bfloat16 [2560, 1024], P(None, 'seq'), may hold values from -0.125 to 0.125
- w_value: bfloat16 [2560, 1024], P(None, 'seq'), may hold values from -0.125 to 0.125
- w_out: bfloat16 [1024, 2560], P('seq'), may hold values from -0.1875 to 0.1875
- w_final: float32 [2560, 64], replicated, may hold values from -0.125 to 0.125
- mod_scale: float32 [2560], replicated, may hold values from -0.9 to 0.9
- mod_shift: float32 [2560], replicated, may hold values from -3 to 3
- skip_gain: float32 [2560], replicated, may hold values from 0.3 to 1.2
Outputs:
- slab_ends: float32 [2, 128, 64], P('slab', ('groups', 'seq')), parts along dimension 1
The draws below stay inside these ranges and needn't reach their ends.
There are 2 independent parts, one for each index of `groups`. The reference program is written for one: setup_inputs(seed, part) draws one part's arguments, and reference() takes and returns one part's arrays. A program takes and returns all parts, laid end to end along the dimension named above; an argument that names none is the same for every part. Nothing has to cross between parts.
Inputs may be any that keep to these rules, and one draw needn't show every extreme that they name: `timesteps`: within a slab the points up to column fine_counts strictly fall; the last used point of a slab is the first point of the next; some slab takes exactly 3 steps.
All inputs are finite; a program needn't handle non-finite values.
Results may differ from the reference program's by a relative error of at most 0.013.
Values may be sent and summed in bfloat16 or wider, within the bound.
A program may use at most 64 MiB of HBM per device.

```python
import math
import jax
import jax.numpy as jnp
from jax import lax

C = 64
D = 2560
HEAD_SIZE = 128
HEADS = 8
TOKENS = 64
FINE_MAX = 3
ITERS = 1
N_SLAB = 2


def plan_draw(seed_key, part):
    base_key = jax.random.fold_in(seed_key, 7)
    split_keys = jax.random.split(base_key, 7)
    slab_ids = jnp.arange(N_SLAB, dtype=jnp.int32)
    offset = jax.random.randint(split_keys[0], (), 0, 4, dtype=jnp.int32)
    code = (jnp.asarray(part).astype(jnp.int32) + offset) % 4
    forced_slab = code // 2 % N_SLAB
    counts_other = 1 + (code + slab_ids) % (FINE_MAX - 1)
    step_counts = jnp.where(slab_ids == forced_slab, FINE_MAX, counts_other).astype(jnp.int32)
    first_time = 999 - jax.random.randint(split_keys[2], (), 0, 20, dtype=jnp.int32)
    last_time = jax.random.randint(split_keys[3], (), 0, 20, dtype=jnp.int32)
    gap_weights = jax.random.randint(split_keys[4], (N_SLAB,), 2, 5, dtype=jnp.int32)
    gap_cumul = jnp.concatenate([jnp.zeros((1,), jnp.int32), jnp.cumsum(gap_weights).astype(jnp.int32)])
    bounds = first_time - (first_time - last_time) * gap_cumul // gap_cumul[-1]
    increments = jax.random.randint(split_keys[5], (N_SLAB, FINE_MAX), 1, 4, dtype=jnp.int32)
    inc_cumul = jnp.concatenate([jnp.zeros((N_SLAB, 1), jnp.int32), jnp.cumsum(increments, axis=1).astype(jnp.int32)], axis=1)
    position = jnp.arange(FINE_MAX + 1, dtype=jnp.int32)[None, :]
    live_total = jnp.sum(jnp.where(position == step_counts[:, None], inc_cumul, 0), axis=1)
    upper = bounds[:-1][:, None]
    lower = bounds[1:][:, None]
    inside = upper - (upper - lower) * inc_cumul // live_total[:, None]
    filler = jax.random.randint(split_keys[6], (N_SLAB, FINE_MAX + 1), 0, 1000, dtype=jnp.int32)
    plan = jnp.where(position <= step_counts[:, None], inside, filler).astype(jnp.int32)
    return (step_counts, plan)


def draw_fine_counts(key, part):
    return plan_draw(key, part)[0]


def draw_timesteps(key, part):
    return plan_draw(key, part)[1]


def draw_w_query(key, part):
    base_key = jax.random.fold_in(key, 11)
    first_key = jax.random.fold_in(base_key, 0)
    entries = jax.random.normal(first_key, (D, HEADS * HEAD_SIZE), jnp.float32) * D ** (-0.5)
    return jnp.clip(entries, -24.0, 24.0).astype(jnp.bfloat16)


def block_scale(key, shape, pieces, low, largest):
    factor_of, own = 1.0, jax.random.fold_in(key, 6)
    for dim, parts in pieces:
        steps = jnp.exp(jax.random.uniform(jax.random.fold_in(own, dim), (parts,), jnp.float32, low / len(pieces), largest / len(pieces)))
        factor_of = factor_of * jnp.repeat(steps, shape[dim] // parts).reshape([-1 if axis == dim else 1 for axis in range(len(shape))])
    return factor_of


def gaussian(own_key, dims, scale, bound, cuts=(), held_as=jnp.bfloat16):
    array = jax.random.normal(own_key, dims, jnp.float32) * scale
    if len(cuts) > 0:
        array = block_scale(own_key, dims, cuts, -0.22, 0.18) * array
    return jnp.clip(array, min=-bound, max=bound).astype(held_as)


def setup_inputs(seed: int = 0, part: int = 0) -> dict:
    arg_keys = jax.random.split(jax.random.key(seed), 13)
    part_keys = jax.random.split(jax.random.fold_in(arg_keys[12], part), 13)
    noise = gaussian(part_keys[0], (TOKENS, C), 1.0, 6.0, ((0, 8),), jnp.float32)
    timesteps = draw_timesteps(jax.random.fold_in(jax.random.fold_in(arg_keys[12], part), 71), part)
    fine_counts = draw_fine_counts(jax.random.fold_in(jax.random.fold_in(arg_keys[12], part), 71), part)
    w_in = gaussian(arg_keys[3], (C, D), C ** -0.5, 0.75)
    w_query = draw_w_query(jax.random.fold_in(arg_keys[12], 71), part)
    w_key = gaussian(arg_keys[5], (D, HEADS * HEAD_SIZE), D ** -0.5, 0.125, ((1, 8),))
    w_value = gaussian(arg_keys[6], (D, HEADS * HEAD_SIZE), D ** -0.5, 0.125, ((1, 8),))
    w_out = gaussian(arg_keys[7], (HEADS * HEAD_SIZE, D), (HEADS * HEAD_SIZE) ** -0.5, 0.1875, ((0, 8),))
    w_final = gaussian(arg_keys[8], (D, C), D ** -0.5, 0.125, (), jnp.float32)
    mod_scale = jnp.clip(jax.random.uniform(arg_keys[9], (D,), jnp.float32, -0.9, 0.9), -0.9, 0.9)
    mod_shift = gaussian(arg_keys[10], (D,), 0.6, 3.0, (), jnp.float32)
    skip_gain = jnp.clip(jax.random.uniform(arg_keys[11], (D,), jnp.float32, 0.3, 1.2), 0.3, 1.2)
    return {"noise": noise, "timesteps": timesteps, "fine_counts": fine_counts, "w_in": w_in, "w_query": w_query, "w_key": w_key, "w_value": w_value, "w_out": w_out, "w_final": w_final, "mod_scale": mod_scale, "mod_shift": mod_shift, "skip_gain": skip_gain}


def attend(queries, key_rows, value_rows, head_size):
    row_total, col_count = queries.shape
    head_count = col_count // head_size
    block_rows = min(512, row_total)
    score_scale = 1.0 / math.sqrt(head_size)

    def split_heads(matrix):
        return matrix.reshape(row_total, head_count, head_size).transpose(1, 0, 2)

    def one_head(triple):
        head_query, head_key, head_value = triple
        blocked = head_query.reshape(row_total // block_rows, block_rows, head_size)

        def one_block(query_block):
            scores = jnp.dot(query_block, head_key.T, preferred_element_type=jnp.float32) * score_scale
            row_top = lax.optimization_barrier(jnp.max(scores, axis=-1, keepdims=True))
            raised = jnp.exp(scores - row_top)
            weights = (raised / lax.optimization_barrier(jnp.sum(raised, axis=-1, keepdims=True))).astype(jnp.bfloat16)
            return jnp.dot(weights, head_value, preferred_element_type=jnp.float32).astype(jnp.bfloat16)
        return lax.map(one_block, blocked).reshape(row_total, head_size)
    merged = lax.map(one_head, (split_heads(queries), split_heads(key_rows), split_heads(value_rows)))
    return merged.transpose(1, 0, 2).reshape(row_total, col_count)

def velocity(latent, noise_level, params):
    w_in, w_query, w_key, w_value, w_out, w_final, mod_scale, mod_shift, skip_gain = params
    hidden = jnp.dot(latent.astype(jnp.bfloat16), w_in, preferred_element_type=jnp.float32)
    squares = lax.optimization_barrier(jnp.mean(hidden * hidden, axis=-1, keepdims=True))
    normed = hidden * lax.rsqrt(squares + 1e-06)
    modulated = (normed * (1.0 + noise_level * mod_scale) + noise_level * mod_shift).astype(jnp.bfloat16)
    queries = jnp.dot(modulated, w_query, preferred_element_type=jnp.float32).astype(jnp.bfloat16)
    key_rows = jnp.dot(modulated, w_key, preferred_element_type=jnp.float32).astype(jnp.bfloat16)
    value_rows = jnp.dot(modulated, w_value, preferred_element_type=jnp.float32).astype(jnp.bfloat16)
    attended = attend(queries, key_rows, value_rows, HEAD_SIZE)
    mixed = jnp.dot(attended, w_out, preferred_element_type=jnp.float32) + skip_gain * normed
    return jnp.dot(mixed, w_final, precision=lax.Precision.HIGHEST, preferred_element_type=jnp.float32)

def reference(noise, timesteps, fine_counts, w_in, w_query, w_key, w_value, w_out, w_final, mod_scale, mod_shift, skip_gain):
    params = (w_in, w_query, w_key, w_value, w_out, w_final, mod_scale, mod_shift, skip_gain)
    sigmas = timesteps.astype(jnp.float32) / 1000.0
    columns = jnp.arange(FINE_MAX + 1).astype(jnp.int32)

    def coarse(latent, slab_id):
        final_level = jnp.sum(jnp.where(columns == fine_counts[slab_id], sigmas[slab_id], 0.0))
        return latent + (final_level - sigmas[slab_id, 0]) * velocity(latent, sigmas[slab_id, 0], params)

    def fine(latent, slab_id):
        for fine_step in range(FINE_MAX):
            step_size = jnp.where(fine_step < fine_counts[slab_id], sigmas[slab_id, fine_step + 1] - sigmas[slab_id, fine_step], 0.0)
            latent = latent + step_size * velocity(latent, sigmas[slab_id, fine_step], params)
        return latent
    first_coarse = coarse(noise, 0)
    starts = [noise]
    for slab_id in range(N_SLAB - 1):
        starts.append(first_coarse if slab_id == 0 else coarse(starts[slab_id], slab_id))
    slab_list = []
    for outer in range(ITERS):
        corrections = []
        for slab_id in range(N_SLAB):
            coarse_old = first_coarse if slab_id == 0 else coarse(starts[slab_id], slab_id)
            corrections.append(fine(starts[slab_id], slab_id) - coarse_old)
        fresh = [noise]
        slab_list = []
        for slab_id in range(N_SLAB):
            coarse_new = first_coarse if slab_id == 0 else coarse(fresh[slab_id], slab_id)
            ended = coarse_new + corrections[slab_id]
            slab_list.append(ended)
            if slab_id + 1 < N_SLAB:
                fresh.append(ended)
        starts = fresh
    return jnp.stack(slab_list)
```

```python
import functools
import math

import jax
import jax.numpy as jnp
from jax import lax
from jax.experimental import pallas as pl
from jax.experimental.pallas import tpu as pltpu
from jax.sharding import PartitionSpec as P

HEAD_SIZE = 128
MESH = pl.DeviceIdType.MESH
BF16 = jnp.bfloat16
F32 = jnp.float32


def two_parts(value):
    high = value.astype(BF16)
    return high, (value - high.astype(F32)).astype(BF16)


def dot(left, right):
    return jnp.dot(left, right, preferred_element_type=F32)


def dot_rows(left, right):
    return lax.dot_general(left, right, (((1,), (1,)), ((), ())), preferred_element_type=F32)


def kernel(
    n,
    times_hbm,
    counts_hbm,
    noise_hbm,
    w_in_hbm,
    w_query_hbm,
    w_key_hbm,
    w_value_hbm,
    w_out_hbm,
    w_final_hbm,
    mod_scale_hbm,
    mod_shift_hbm,
    skip_gain_hbm,
    out,
    times,
    counts,
    noise_here,
    lift_rows,
    projections,
    final_rows,
    final_map,
    final_parts,
    mod_scale,
    mod_shift,
    skip_gain,
    noise_stage,
    noise_all,
    share_stage,
    pair_shares,
    shares,
    end_stage,
    ends,
    latent_end,
    copy_sems,
    noise_send,
    noise_recv,
    pair_send,
    pair_recv,
    share_send,
    share_recv,
    end_send,
    end_recv,
):
    me = lax.axis_index("seq")
    slab = lax.axis_index("slab")
    fine_most = times.shape[1] - 1
    rows, channels = noise_here.shape
    half = n // 2
    slot = lax.rem(me, half)
    packed = half * rows
    tokens = n * rows
    width = w_in_hbm.shape[1]
    cols = w_query_hbm.shape[1]
    heads = cols // HEAD_SIZE
    lanes = 2 * channels

    def peer(step):
        return lax.rem(me + step, n)

    fetches = [
        (noise_hbm, noise_here),
        (w_in_hbm, lift_rows.at[pl.ds(0, channels)]),
        (mod_scale_hbm, mod_scale.at[0]),
        (mod_shift_hbm, mod_shift.at[0]),
        (skip_gain_hbm, skip_gain.at[0]),
        (w_query_hbm, projections.at[:, pl.ds(0, cols)]),
        (w_key_hbm, projections.at[:, pl.ds(cols, cols)]),
        (w_value_hbm, projections.at[:, pl.ds(2 * cols, cols)]),
        (w_final_hbm, final_map),
        (w_out_hbm, final_rows.at[pl.ds(0, cols)]),
        (w_in_hbm, final_rows.at[pl.ds(cols + lanes, channels)]),
        (w_in_hbm, final_parts.at[pl.ds(lanes, channels)]),
        (w_in_hbm, final_parts.at[pl.ds(lanes + channels, channels)]),
        (times_hbm, times),
        (counts_hbm, counts),
    ]
    copies = [
        pltpu.make_async_copy(source, target, copy_sems.at[index])
        for index, (source, target) in enumerate(fetches)
    ]
    barrier = pltpu.get_barrier_semaphore()
    for copy in copies:
        copy.start()
    for other in range(2):
        for step in range(n):
            if other or step:
                pl.semaphore_signal(
                    barrier,
                    inc=1,
                    device_id={"seq": peer(step), "slab": lax.rem(slab + other, 2)},
                    device_id_type=MESH,
                )

    copies[0].wait()
    tile = noise_here[...]
    tile = jnp.concatenate([tile, tile], axis=1)
    noise_stage[...] = tile
    noise_all[me] = tile
    pl.semaphore_wait(barrier, 2 * n - 1)
    for step in range(1, n):
        pltpu.make_async_remote_copy(
            src_ref=noise_stage,
            dst_ref=noise_all.at[me],
            send_sem=noise_send,
            recv_sem=noise_recv,
            device_id={"seq": peer(step)},
            device_id_type=MESH,
        ).start()

    def all_of(buffer, send_sem, recv_sem):
        return pltpu.make_async_remote_copy(
            src_ref=buffer,
            dst_ref=buffer,
            send_sem=send_sem,
            recv_sem=recv_sem,
            device_id={"seq": peer(1)},
            device_id_type=MESH,
        )

    copies[13].wait()
    copies[14].wait()
    sigma = [
        [times[k, j].astype(F32) * (1.0 / 1000.0) for j in range(fine_most + 1)] for k in range(2)
    ]
    size = [
        [
            jnp.where(j < counts[k], sigma[k][j + 1] - sigma[k][j], 0.0)
            for j in range(fine_most)
        ]
        for k in range(2)
    ]
    coarse = []
    for k in range(2):
        last = sigma[k][0]
        for j in range(1, fine_most + 1):
            last = jnp.where(counts[k] == j, sigma[k][j], last)
        coarse.append(last - sigma[k][0])
    first = slab == 0
    levels = [sigma[0][0]]
    sizes = [jnp.where(first, size[0][0], coarse[0])]
    for j in range(1, fine_most):
        levels.append(jnp.where(first, sigma[0][j], sigma[1][j - 1]))
        sizes.append(jnp.where(first, size[0][j], size[1][j - 1]))
    levels.append(jnp.where(first, sigma[1][0], sigma[1][fine_most - 1]))
    sizes.append(jnp.where(first, coarse[1], size[1][fine_most - 1]))

    for copy in copies[1:5]:
        copy.wait()
    w_in = lift_rows[pl.ds(0, channels), :].astype(F32)
    high, low = two_parts(w_in * mod_scale[...])
    lift_rows[pl.ds(channels, channels), :] = high
    lift_rows[pl.ds(2 * channels, channels), :] = low
    shift_high, shift_low = two_parts(mod_shift[...])
    row_id = lax.broadcasted_iota(jnp.int32, (16, width), 0)
    lift_rows[pl.ds(3 * channels, 16), :] = jnp.where(
        row_id == 0,
        shift_high.astype(F32),
        jnp.where(row_id == 1, shift_low.astype(F32), 0.0),
    ).astype(BF16)
    high, low = two_parts(w_in * skip_gain[...])
    final_rows[pl.ds(cols, channels), :] = high
    final_rows[pl.ds(cols + channels, channels), :] = low
    for copy in copies[5:8]:
        copy.wait()
    lifted = dot(lift_rows[...], projections[...])
    terms = jnp.concatenate(
        [
            lifted[:channels],
            lifted[channels : 2 * channels] + lifted[2 * channels : 3 * channels],
            jnp.broadcast_to(
                lifted[3 * channels : 3 * channels + 1] + lifted[3 * channels + 1 : 3 * channels + 2],
                (16, 3 * cols),
            ),
        ],
        axis=0,
    )

    for copy in copies[8:13]:
        copy.wait()
    high, low = two_parts(final_map[...])
    final_parts[pl.ds(0, channels), :] = high
    final_parts[pl.ds(channels, channels), :] = low
    folded = dot_rows(final_rows[...], final_parts[...])
    gram = folded[cols + lanes :, lanes:]
    folded = folded[: cols + lanes, :lanes]
    folded = folded + pltpu.roll(folded, channels, axis=1)
    left = lax.broadcasted_iota(jnp.int32, (1, lanes), 1) < channels
    nothing = jnp.zeros((1, lanes), F32)

    def beside(value):
        return jnp.concatenate(
            [jnp.where(left, value, nothing), jnp.where(left, nothing, value)], axis=0
        )

    skip_high, skip_low = two_parts(
        beside(folded[cols : cols + channels] + folded[cols + channels : cols + 2 * channels])
    )
    skip_map = jnp.concatenate([skip_high, skip_low], axis=0)

    values = []
    for h in range(heads):
        at = 2 * cols + h * HEAD_SIZE
        high, low = two_parts(terms[:, at : at + HEAD_SIZE])
        map_high, map_low = two_parts(folded[h * HEAD_SIZE : (h + 1) * HEAD_SIZE])
        values.append(dot(high, map_high) + dot(low, map_high) + dot(high, map_low))
    terms = jnp.concatenate(
        [
            terms[:, :cols] * (math.log2(math.e) / math.sqrt(HEAD_SIZE)),
            terms[:, cols : 2 * cols],
            *values,
        ],
        axis=1,
    )
    plain, scaled, shift = (
        terms[:channels],
        terms[channels : 2 * channels],
        terms[2 * channels : 2 * channels + 1],
    )
    gram_high, gram_mid = two_parts(gram)
    gram_low = (gram - gram_high.astype(F32) - gram_mid.astype(F32)).astype(BF16).astype(F32)
    gram_top = jnp.where(left, gram_high.astype(F32), gram_low).astype(BF16)
    gram_below = jnp.where(left, gram_mid.astype(F32), nothing).astype(BF16)
    gram_map = jnp.concatenate([gram_top, gram_top, gram_below, gram_below], axis=0)

    def level_map(level):
        high, low = two_parts(plain + level * scaled)
        weights = jnp.concatenate([high, high, low, low], axis=0)
        return jnp.concatenate([weights, gram_map], axis=1), level * shift

    def share_of(latent, mapped, offset):
        rounded = latent.astype(BF16).astype(F32)
        apart = beside(rounded).astype(BF16)
        turned = pltpu.roll(rounded, channels, axis=1)
        both = jnp.concatenate(
            [jnp.where(left, rounded, turned), jnp.where(left, turned, rounded)], axis=0
        )
        lifted = dot(jnp.concatenate([apart, apart], axis=1), mapped)
        squares = jnp.sum(lifted[:, -lanes:] * both, axis=-1, keepdims=True)
        inverse = lax.rsqrt(jnp.maximum(squares, 0.0) * (1.0 / width) + 1e-06)
        joined = (lifted[:, :-lanes] * inverse + offset).astype(BF16)
        share = jnp.zeros((packed, lanes), F32)
        blank = jnp.zeros((tokens, HEAD_SIZE), BF16)
        for h in range(heads):
            at = h * HEAD_SIZE
            query = joined[:, at : at + HEAD_SIZE]
            key = joined[:, cols + at : cols + at + HEAD_SIZE]
            value = joined[:, 2 * cols + h * lanes : 2 * cols + (h + 1) * lanes].astype(F32)
            scores = dot_rows(
                jnp.concatenate([query[:packed], query[packed:]], axis=1),
                jnp.concatenate(
                    [
                        jnp.concatenate([key, blank], axis=1),
                        jnp.concatenate([blank, key], axis=1),
                    ],
                    axis=0,
                ),
            )
            in_first = lax.broadcasted_iota(jnp.int32, (1, 2 * tokens), 1) < tokens
            top = jnp.where(
                in_first,
                jnp.max(jnp.where(in_first, scores, -jnp.inf), axis=-1, keepdims=True),
                jnp.max(jnp.where(in_first, -jnp.inf, scores), axis=-1, keepdims=True),
            )
            raised = jnp.exp2(scores - top).astype(BF16)
            ones = jnp.ones((tokens, lanes), F32)
            result = dot(
                raised, jnp.concatenate([beside(value), beside(ones)], axis=1).astype(BF16)
            )
            share = share + result[:, :lanes] / result[:, lanes:]
        pair = jnp.where(left, inverse[:packed], inverse[packed:])
        return share, (rounded.astype(BF16), pair)

    def skip_of(kept):
        rounded, pair = kept
        return pair * dot(jnp.concatenate([rounded, rounded], axis=1), skip_map)

    mapped, offset = level_map(levels[0])
    all_of(noise_all.at[pl.ds(0, n - 1)], noise_send, noise_recv).wait_recv()
    latent = jnp.concatenate(
        [jnp.where(left, noise_all[t], noise_all[t + half]) for t in range(half)], axis=0
    )
    change = jnp.zeros((packed, lanes), F32)
    for step in range(fine_most):
        share, kept = share_of(latent, mapped, offset)
        share = share.astype(BF16)
        share_stage[step] = share
        pltpu.make_async_remote_copy(
            src_ref=share_stage.at[step],
            dst_ref=pair_shares.at[step],
            send_sem=pair_send.at[step],
            recv_sem=pair_recv.at[step],
            device_id={"seq": peer(half)},
            device_id_type=MESH,
        ).start()
        velocity = skip_of(kept)
        all_of(pair_shares.at[step], pair_send.at[step], pair_recv.at[step]).wait_recv()
        shares[step, slot] = (share.astype(F32) + pair_shares[step].astype(F32)).astype(BF16)
        for off in range(1, half):
            pltpu.make_async_remote_copy(
                src_ref=shares.at[step, slot],
                dst_ref=shares.at[step, slot],
                send_sem=share_send.at[step],
                recv_sem=share_recv.at[step],
                device_id={"seq": me - slot + lax.rem(slot + off, half)},
                device_id_type=MESH,
            ).start()
        mapped, offset = level_map(levels[step + 1])
        all_of(
            shares.at[step, pl.ds(0, half - 1)], share_send.at[step], share_recv.at[step]
        ).wait_recv()
        for index in range(half):
            velocity = velocity + shares[step, index].astype(F32)
        latent = latent + sizes[step] * velocity
        if step == 1:
            change = (sizes[step] - coarse[1]) * velocity
        elif step > 1:
            change = change + sizes[step] * velocity

    latent_end[...] = latent
    share, kept = share_of(latent, mapped, offset)
    row_owner = lax.broadcasted_iota(jnp.int32, (packed, lanes), 0) // rows
    lane_owner = lax.broadcasted_iota(jnp.int32, (packed, lanes), 1) // channels
    own = (row_owner + half * lane_owner) == me
    base = jnp.where(first, latent, change) + sizes[fine_most] * skip_of(kept)
    end_stage[...] = sizes[fine_most] * share + jnp.where(own, base, 0.0)
    place = slab * n + me

    def send_end(target):
        start = pl.multiple_of(lax.rem(target, half) * rows, rows)
        pltpu.make_async_remote_copy(
            src_ref=end_stage.at[pl.ds(start, rows)],
            dst_ref=ends.at[place],
            send_sem=end_send,
            recv_sem=end_recv,
            device_id={"seq": target, "slab": 1},
            device_id_type=MESH,
        ).start()

    for off in range(1, n):
        send_end(peer(off))

    my_rows = pl.ds(pl.multiple_of(lax.rem(me, half) * rows, rows), rows)
    in_left = me < half

    def mine(value):
        return jnp.where(in_left, value[:, :channels], value[:, channels:])

    @pl.when(first)
    def _():
        send_end(me)
        out[0] = mine(latent_end[my_rows, :])
        all_of(ends.at[pl.ds(0, n)], end_send, end_recv).wait_send()

    @pl.when(slab == 1)
    def _():
        ends[place] = end_stage[my_rows, :]
        all_of(ends.at[pl.ds(0, 2 * n - 1)], end_send, end_recv).wait_recv()
        total = ends[0]
        for index in range(1, 2 * n):
            total = total + ends[index]
        out[0] = mine(total)
        all_of(ends.at[pl.ds(0, n - 1)], end_send, end_recv).wait_send()

    all_of(noise_all.at[pl.ds(0, n - 1)], noise_send, noise_recv).wait_send()
    for step in range(fine_most):
        all_of(pair_shares.at[step], pair_send.at[step], pair_recv.at[step]).wait_send()
        all_of(
            shares.at[step, pl.ds(0, half - 1)], share_send.at[step], share_recv.at[step]
        ).wait_send()


def local(
    noise,
    timesteps,
    fine_counts,
    w_in,
    w_query,
    w_key,
    w_value,
    w_out,
    w_final,
    mod_scale,
    mod_shift,
    skip_gain,
):
    n = lax.axis_size("seq")
    if lax.axis_size("slab") != 2 or n % 2 or n < 4:
        raise ValueError("unsupported mesh")
    rows, channels = noise.shape
    width = w_in.shape[1]
    cols = w_query.shape[1]
    fine_most = timesteps.shape[1] - 1
    lanes = 2 * channels
    packed = n // 2 * rows
    anywhere = pl.BlockSpec(memory_space=pl.ANY)
    dma = pltpu.SemaphoreType.DMA
    return pl.pallas_call(
        functools.partial(kernel, n),
        out_shape=pltpu.VMEM((1, rows, channels), F32),
        in_specs=[anywhere] * 12,
        out_specs=pl.BlockSpec(memory_space=pltpu.VMEM),
        scratch_shapes=[
            pltpu.SMEM(timesteps.shape, jnp.int32),
            pltpu.SMEM(fine_counts.shape, jnp.int32),
            pltpu.VMEM((rows, channels), F32),
            pltpu.VMEM((3 * channels + 16, width), BF16),
            pltpu.VMEM((width, 3 * cols), BF16),
            pltpu.VMEM((cols + lanes + channels, width), BF16),
            pltpu.VMEM((channels, width), F32),
            pltpu.VMEM((2 * lanes, width), BF16),
            pltpu.VMEM((1, width), F32),
            pltpu.VMEM((1, width), F32),
            pltpu.VMEM((1, width), F32),
            pltpu.VMEM((rows, lanes), F32),
            pltpu.VMEM((n, rows, lanes), F32),
            pltpu.VMEM((fine_most, packed, lanes), BF16),
            pltpu.VMEM((fine_most, packed, lanes), BF16),
            pltpu.VMEM((fine_most, n // 2, packed, lanes), BF16),
            pltpu.VMEM((packed, lanes), F32),
            pltpu.VMEM((2 * n, rows, lanes), F32),
            pltpu.VMEM((packed, lanes), F32),
            dma((15,)),
            dma,
            dma,
            dma((fine_most,)),
            dma((fine_most,)),
            dma((fine_most,)),
            dma((fine_most,)),
            dma,
            dma,
        ],
        compiler_params=pltpu.CompilerParams(
            collective_id=0, has_side_effects=True, vmem_limit_bytes=60 * 1024 * 1024
        ),
    )(
        timesteps,
        fine_counts,
        noise,
        w_in,
        w_query,
        w_key,
        w_value,
        w_out,
        w_final.T,
        mod_scale,
        mod_shift,
        skip_gain,
    )


def solution(mesh):
    placed = (
        P(("groups", "seq"), None),
        P("groups", None),
        P("groups"),
        P(),
        P(None, "seq"),
        P(None, "seq"),
        P(None, "seq"),
        P("seq", None),
        P(),
        P(),
        P(),
        P(),
    )
    return jax.shard_map(
        local,
        mesh=mesh,
        in_specs=placed,
        out_specs=P("slab", ("groups", "seq"), None),
        check_vma=False,
    )
```
